32 devices in a mesh: grp: 2 (over y), exp: 4 (over z), rep: 4 (over x, core).
Axes of the slice: x: 2, y: 2, z: 4, core: 2. Of those that a mesh axis runs over, the one named last changes fastest.
Arguments:
- tokens: bfloat16 [4096, 1024], P(('grp', 'exp', 'rep')), parts along dimension 0, may hold values from -6 to 6
- routes: int32 [4096, 2], P(('grp', 'exp', 'rep')), parts along dimension 0, may hold values from 0 to 7, all different within a row; in each aligned block of 128 rows (0 to 127, 128 to 255, ...) at most 48 rows name the same one
- combine: float32 [4096, 2], P(('grp', 'exp', 'rep')), parts along dimension 0, may hold values from 0.2 to 1
- w_gate: bfloat16 [8, 1024, 2048], P('exp', None, 'rep'), may hold values from -0.1875 to 0.1875
- w_up: bfloat16 [8, 1024, 2048], P('exp', None, 'rep'), may hold values from -0.1875 to 0.1875
- w_down: bfloat16 [8, 2048, 1024], P('exp', 'rep'), may hold values from -0.125 to 0.125
Outputs:
- expert_mix: bfloat16 [4096, 1024], P(('grp', 'exp', 'rep')), parts along dimension 0
The draws below stay inside these ranges and needn't reach their ends.
There are 2 independent parts, one for each index of `grp`. The reference program is written for one: setup_inputs(seed, part) draws one part's arguments, and reference() takes and returns one part's arrays. A program takes and returns all parts, laid end to end along the dimension named above; an argument that names none is the same for every part. Nothing has to cross between parts.
Inputs may be any that keep to these rules, and one draw needn't show every extreme that they name: `routes`: each row names 2 different experts. Within the 128 tokens of one device no expert is named more than 48 times, a bound that some block reaches.
All inputs are finite; a program needn't handle non-finite values.
Results may differ from the reference program's by a relative error of at most 0.0078.
Values may be sent and summed in bfloat16 or wider, within the bound.
A program may use at most 64 MiB of HBM per device.

```python
import math
import jax
import jax.numpy as jnp
import numpy as np
from jax import lax

D = 1024
FF = 2048
TOP = 2
TOK_DEV = 128
EXPERTS = 8
CAP = 48
TOKENS = 2048
N_REP = 4


def level_of(rng, extent, pieces, low, largest):
    level, own = 1.0, jax.random.fold_in(rng, 6)
    for axis_at, shards_of in pieces:
        draws = jnp.exp(jax.random.uniform(jax.random.fold_in(own, axis_at), (shards_of,), jnp.float32, low / len(pieces), largest / len(pieces)))
        level = level * jnp.repeat(draws, extent[axis_at] // shards_of).reshape([-1 if axis == axis_at else 1 for axis in range(len(extent))])
    return level


def shared_out(stream_key, own, number, rows, count, top, most, slope):
    sequence = jax.random.permutation(stream_key, count)
    packed, usual = load_shares(count, rows * top, most, slope, True), load_shares(count, rows * top, most, slope, False)
    places = jnp.arange(count)

    def named(tallies, offset_by):
        used = int((tallies > 0).sum())
        fixed = max(1, used // 4)
        moved = fixed + (places - fixed + offset_by * (used - fixed)) % max(1, count - fixed)
        return jnp.zeros((count,), jnp.int32).at[sequence[jnp.where(places < fixed, places, moved)]].set(jnp.asarray(tallies, jnp.int32))

    tallies = jnp.where(number % 4 == 0, named(packed, number // 4), named(usual, number - number // 4 - 1))
    mixed = jax.random.permutation(jax.random.fold_in(own, 3), count)
    source_of, taker = mixed[0:count // 2 * 2:2], mixed[1:count // 2 * 2:2]
    room = jnp.minimum(tallies[source_of] - 1, most - tallies[taker]) // 2
    room = jnp.where((source_of == sequence[0]) | (taker == sequence[0]) | (tallies[taker] == 0), 0, jnp.maximum(room, 0))
    moved = jax.random.randint(jax.random.fold_in(own, 4), (count // 2,), 0, 1 << 20) % (room + 1)
    tallies = tallies.at[source_of].add(-moved).at[taker].add(moved)
    items = jnp.searchsorted(jnp.cumsum(tallies), jnp.arange(rows * top), side="right").astype(jnp.int32)
    listing = items.reshape(top, rows).T
    listing = listing[jax.random.permutation(jax.random.fold_in(own, 1), rows)]
    offset_by = jax.random.randint(jax.random.fold_in(own, 2), (rows, 1), 0, top)
    return jnp.take_along_axis(listing, (jnp.arange(top)[None, :] + offset_by) % top, axis=1)


def load_shares(count, total, most, slope, full):
    weights = [(1 << 20) // math.isqrt(rank ** slope) + 1 for rank in range(1, count + 1)]
    largest = most if full else min(most, max(-(-total // count), total * weights[0] // sum(weights)))
    least = 1 if total - largest >= count - 1 else 0
    counts, rest = [largest] + [least] * (count - 1), total - largest - least * (count - 1)
    while rest > 0:
        movable = [i for i in range(1, count) if counts[i] < largest] or [i for i in range(1, count) if counts[i] < most]
        whole, left = sum([weights[i] for i in movable]), rest
        for i in movable:
            extra = min(most - counts[i], max(1, left * weights[i] // whole), rest)
            counts[i] = counts[i] + extra
            rest = rest - extra
    return np.array(counts)


def scatter_about(stream_key, dims, scale, bound, shards=(), held_as=jnp.bfloat16):
    level = level_of(stream_key, dims, shards, -0.22, 0.18) if shards else 1.0
    values = jax.random.normal(stream_key, dims, jnp.float32) * scale * level
    return jnp.minimum(jnp.maximum(values, -bound), bound).astype(held_as)


def setup_inputs(seed: int = 0, part: int = 0) -> dict:
    seeds = jax.random.split(jax.random.key(seed), 7)
    own_keys = jax.random.split(jax.random.fold_in(seeds[6], part), 7)
    tokens = scatter_about(own_keys[0], (TOKENS, D), 1.0, 6.0, ((0, 16),))
    routes_keys = jax.random.split(jax.random.fold_in(own_keys[1], 1), TOKENS // TOK_DEV)
    routes_turns = jax.random.permutation(jax.random.fold_in(own_keys[1], 3), TOKENS // TOK_DEV)
    routes = jax.vmap(lambda own, number: shared_out(jax.random.fold_in(own_keys[1], 2), own, number, TOK_DEV, EXPERTS, TOP, CAP, 2))(routes_keys, routes_turns).reshape((TOKENS, TOP))
    combine = jnp.clip(0.2 + 0.8 * jax.random.uniform(own_keys[2], (TOKENS, TOP), jnp.float32) ** level_of(own_keys[2], (TOKENS, TOP), ((0, 16),), -0.2, 0.2), 0.2, 1.0)
    w_gate = scatter_about(seeds[3], (EXPERTS, D, FF), D ** -0.5, 0.1875, ((0, 4), (2, 4)))
    w_up = scatter_about(seeds[4], (EXPERTS, D, FF), D ** -0.5, 0.1875, ((0, 4), (2, 4)))
    w_down = scatter_about(seeds[5], (EXPERTS, FF, D), FF ** -0.5, 0.125, ((0, 4), (1, 4)))
    return {"tokens": tokens, "routes": routes, "combine": combine, "w_gate": w_gate, "w_up": w_up, "w_down": w_down}


def reference(tokens, routes, combine, w_gate, w_up, w_down):
    blocks = TOKENS // TOK_DEV
    values = tokens.astype(jnp.float32)
    normed = (values * lax.rsqrt(lax.optimization_barrier(jnp.mean(values * values, axis=-1, keepdims=True)) + 1e-05)).astype(jnp.bfloat16)
    chosen = routes.reshape(blocks, TOK_DEV * TOP)
    onehot = (chosen[:, :, None] == jnp.arange(EXPERTS, dtype=jnp.int32)[None, None, :]).astype(jnp.int32)
    before = jnp.cumsum(onehot, axis=1) - onehot
    position = lax.optimization_barrier(jnp.sum(before * onehot, axis=-1))
    block_ids = jnp.arange(blocks, dtype=jnp.int32)[:, None]
    where = (chosen * (blocks * CAP) + block_ids * CAP + position).reshape(-1).astype(jnp.int32)
    source = jnp.repeat(normed, TOP, axis=0)
    buffer = jnp.zeros((EXPERTS * blocks * CAP, D), jnp.bfloat16).at[where].set(source)
    buffer = buffer.reshape(EXPERTS, blocks * CAP, D)
    slice_width = FF // N_REP

    def expert_ffn(operands):
        rows, gate_w, up_w, down_w = operands
        gate = jnp.dot(rows, gate_w, preferred_element_type=jnp.float32)
        up = jnp.dot(rows, up_w, preferred_element_type=jnp.float32)
        hidden = (jax.nn.silu(gate) * up).astype(jnp.bfloat16)
        total = jnp.zeros((rows.shape[0], D), jnp.float32)
        for index in range(N_REP):
            partial_sum = jnp.dot(hidden[:, index * slice_width:(index + 1) * slice_width], down_w[index * slice_width:(index + 1) * slice_width], preferred_element_type=jnp.float32)
            rounded = lax.optimization_barrier(partial_sum.astype(jnp.bfloat16))
            total = total + rounded.astype(jnp.float32)
        return total.astype(jnp.bfloat16)
    outputs = lax.map(expert_ffn, (buffer, w_gate, w_up, w_down))
    picked = outputs.reshape(-1, D)[where].reshape(TOKENS, TOP, D)
    mixed = lax.optimization_barrier(jnp.sum(combine[:, :, None] * picked.astype(jnp.float32), axis=1))
    return mixed.astype(jnp.bfloat16)
```

```python
import functools

import jax
import jax.numpy as jnp
from jax import lax
from jax.experimental import pallas as pl
from jax.experimental.pallas import tpu as pltpu
from jax.sharding import PartitionSpec as P

MESH = pl.DeviceIdType.MESH
BF = jnp.bfloat16
F32 = jnp.float32


def kernel(
    K, n, X, cap, S,
    tok_ref, routes_ref, combine_ref, wg_hbm, wu_hbm, wd_hbm, out_ref,
    wg, wu, wd, own, rows, ckeep, csend, crecv, xkeep, xsend, xrecv, zsend, back, picks,
    w_sem, z_s, z_r, x_s, x_r, c_s, c_r, rc_s, rc_r, rx_s, rx_r, rz_s, rz_r,
):
    T = K * n
    D = tok_ref.shape[1]
    tok_rows = tok_ref.shape[0]
    z = lax.axis_index("exp")
    r = lax.axis_index("rep")
    x, c = r // 2, r % 2

    def at_z(o):
        return {"exp": (z + o + n) % n}

    def at_x(o):
        return {"rep": ((x + o + X) % X) * 2 + c}

    sibling = {"rep": x * 2 + 1 - c}

    def remote(src, dst, send, recv, where):
        return pltpu.make_async_remote_copy(
            src_ref=src, dst_ref=dst, send_sem=send, recv_sem=recv,
            device_id=where, device_id_type=MESH,
        )

    def z_copy(t, i):
        return remote(own.at[t], rows.at[t, 0, 0], z_s.at[t], z_r.at[t], at_z(-i))

    def x_copy(t, o):
        return remote(rows.at[t, 0, 0], rows.at[t, o, 0], x_s.at[t, o - 1], x_r.at[t, o - 1], at_x(-o))

    def c_copy(t, o):
        return remote(rows.at[t, o, 0], rows.at[t, o, 1], c_s.at[t, o], c_r.at[t, o], sibling)

    def rc_copy(t):
        return remote(csend.at[t], crecv.at[t], rc_s.at[t], rc_r.at[t], sibling)

    def rx_copy(t, o):
        return remote(xsend.at[t, o - 1], xrecv.at[t, o - 1], rx_s.at[t, o - 1], rx_r.at[t, o - 1], at_x(o))

    def rz_copy(t, i):
        return remote(zsend.at[t], back.at[t], rz_s.at[t], rz_r.at[t], at_z(i))

    def w_copies(k):
        return [
            pltpu.make_async_copy(src.at[k], dst.at[k], w_sem.at[m, k])
            for m, (src, dst) in enumerate(((wg_hbm, wg), (wu_hbm, wu), (wd_hbm, wd)))
        ]

    barrier = pltpu.get_barrier_semaphore()
    for o in range(1, n):
        pl.semaphore_signal(barrier, inc=1, device_id=at_z(o), device_id_type=MESH)
    for o in range(1, X):
        pl.semaphore_signal(barrier, inc=1, device_id=at_x(o), device_id_type=MESH)
    pl.semaphore_signal(barrier, inc=1, device_id=sibling, device_id_type=MESH)

    for k in range(K):
        for copy in w_copies(k):
            copy.start()

    values = tok_ref[...].astype(F32)
    scale = lax.rsqrt(jnp.mean(values * values, axis=-1, keepdims=True) + 1e-05)
    normed = (values * scale).astype(BF)
    experts = n * K
    lanes = max(128, experts)
    expert_ids = lax.broadcasted_iota(jnp.int32, (tok_rows, lanes), 1)
    hot = [(routes_ref[:, j : j + 1] == expert_ids).astype(F32) for j in range(2)]
    tri = (
        lax.broadcasted_iota(jnp.int32, (tok_rows, tok_rows), 1)
        < lax.broadcasted_iota(jnp.int32, (tok_rows, tok_rows), 0)
    ).astype(F32).astype(BF)
    before = jnp.dot(tri, (hot[0] + hot[1]).astype(BF), preferred_element_type=F32)
    slot_ids = lax.broadcasted_iota(jnp.int32, (tok_rows, T * S), 1)
    table = []
    for j in range(2):
        position = jnp.sum(before * hot[j], axis=1, keepdims=True).astype(jnp.int32)
        e = routes_ref[:, j : j + 1]
        ze = lax.div(e, jnp.full_like(e, K))
        ke = e - ze * K
        ie = z - ze
        ie = jnp.where(ie < 0, ie + n, ie)
        slot = (ke * n + ie) * S + position
        table.append((slot == slot_ids).astype(F32))
        picks[j] = table[j].astype(BF)
    sent = lax.dot_general(
        (table[0] + table[1]).astype(BF), normed, (((0,), (0,)), ((), ())), preferred_element_type=F32
    ).astype(BF).reshape(T, S, D)
    own[...] = sent
    for k in range(K):
        rows[k * n, 0, 0] = sent[k * n]

    pl.semaphore_wait(barrier, n + X - 1)
    for k in range(K):
        @pl.loop(1, n)
        def _(i):
            z_copy(k * n + i, i).start()

    def stage_a(t):
        i = t % n

        @pl.when(i > 0)
        def _():
            z_copy(t, i).wait_recv()

        for o in range(1, X):
            x_copy(t, o).start()
        c_copy(t, 0).start()

    def stage_b(t):
        for o in range(1, X):
            x_copy(t, o).wait_recv()
            c_copy(t, o).start()

    def stage_c(t):
        k = t // n

        @pl.when(t % n == 0)
        def _():
            for copy in w_copies(k):
                copy.wait()

        for o in range(X):
            c_copy(t, o).wait_recv()
        a = rows[t].reshape(X * 2 * S, D)
        gate = jnp.dot(a, wg[k], preferred_element_type=F32)
        up = jnp.dot(a, wu[k], preferred_element_type=F32)
        hidden = (gate / (1.0 + jnp.exp(-gate)) * up).astype(BF)
        part = jnp.dot(hidden, wd[k], preferred_element_type=F32).reshape(X, 2, S, D)
        csend[t] = part[:, 1].astype(BF)
        rc_copy(t).start()
        ckeep[t % 2] = part[:, 0]

    def stage_d(t):
        rc_copy(t).wait_recv()
        for o in range(1, X):
            xsend[t, o - 1] = (ckeep[t % 2, o] + crecv[t, o].astype(F32)).astype(BF)
            rx_copy(t, o).start()
        xkeep[t % 2] = ckeep[t % 2, 0] + crecv[t, 0].astype(F32)

    def stage_e(t):
        i = t % n
        total = xkeep[t % 2]
        for o in range(1, X):
            rx_copy(t, o).wait_recv()
            total = total + xrecv[t, o - 1].astype(F32)
        total = total.astype(BF)

        @pl.when(i > 0)
        def _():
            zsend[t] = total
            rz_copy(t, i).start()

        @pl.when(i == 0)
        def _():
            back[t] = total

    stages = ((0, stage_a), (1, stage_b), (4, stage_e), (3, stage_d), (2, stage_c))

    @pl.loop(0, T + 4)
    def _(tick):
        for lag, stage in stages:
            @pl.when((tick >= lag) & (tick < T + lag))
            def _(lag=lag, stage=stage):
                stage(tick - lag)

    for k in range(K):
        @pl.loop(1, n)
        def _(i):
            rz_copy(k * n + i, i).wait_recv()

    landed = back[...].reshape(T * S, D)
    mixed = combine_ref[:, 0:1] * jnp.dot(picks[0], landed, preferred_element_type=F32)
    mixed = mixed + combine_ref[:, 1:2] * jnp.dot(picks[1], landed, preferred_element_type=F32)
    out_ref[...] = mixed.astype(BF)

    @pl.loop(0, T)
    def _(t):
        i = t % n

        @pl.when(i > 0)
        def _():
            z_copy(t, i).wait_send()
            rz_copy(t, i).wait_send()

        for o in range(X):
            c_copy(t, o).wait_send()
        rc_copy(t).wait_send()
        for o in range(1, X):
            x_copy(t, o).wait_send()
            rx_copy(t, o).wait_send()


def body(n, R, tokens, routes, combine, w_gate, w_up, w_down):
    tok_rows, D = tokens.shape
    K, _, F = w_gate.shape
    X = R // 2
    cap = max(2, 3 * tok_rows // (K * n))
    S = -(-cap // 16) * 16
    T = K * n
    vmem = pl.BlockSpec(memory_space=pltpu.VMEM)
    hbm = pl.BlockSpec(memory_space=pl.ANY)
    dma = pltpu.SemaphoreType.DMA
    macs = T * X * 2 * S * D * F * 3
    return pl.pallas_call(
        functools.partial(kernel, K, n, X, cap, S),
        out_shape=jax.ShapeDtypeStruct((tok_rows, D), BF),
        in_specs=[vmem, vmem, vmem, hbm, hbm, hbm],
        out_specs=vmem,
        scratch_shapes=[
            pltpu.VMEM((K, D, F), BF),
            pltpu.VMEM((K, D, F), BF),
            pltpu.VMEM((K, F, D), BF),
            pltpu.VMEM((T, S, D), BF),
            pltpu.VMEM((T, X, 2, S, D), BF),
            pltpu.VMEM((2, X, S, D), F32),
            pltpu.VMEM((T, X, S, D), BF),
            pltpu.VMEM((T, X, S, D), BF),
            pltpu.VMEM((2, S, D), F32),
            pltpu.VMEM((T, X - 1, S, D), BF),
            pltpu.VMEM((T, X - 1, S, D), BF),
            pltpu.VMEM((T, S, D), BF),
            pltpu.VMEM((T, S, D), BF),
            pltpu.VMEM((2, tok_rows, T * S), BF),
            dma((3, K)),
            dma((T,)), dma((T,)),
            dma((T, X - 1)), dma((T, X - 1)),
            dma((T, X)), dma((T, X)),
            dma((T,)), dma((T,)),
            dma((T, X - 1)), dma((T, X - 1)),
            dma((T,)), dma((T,)),
        ],
        compiler_params=pltpu.CompilerParams(
            collective_id=0, has_side_effects=True, vmem_limit_bytes=60 * 1024 * 1024
        ),
        cost_estimate=pl.CostEstimate(flops=2 * macs, bytes_accessed=6 * K * D * F, transcendentals=T * X * 2 * S * F),
    )(tokens, routes, combine, w_gate, w_up, w_down)


def solution(mesh):
    in_specs = (
        P(("grp", "exp", "rep"), None),
        P(("grp", "exp", "rep"), None),
        P(("grp", "exp", "rep"), None),
        P("exp", None, "rep"),
        P("exp", None, "rep"),
        P("exp", "rep", None),
    )
    out_specs = P(("grp", "exp", "rep"), None)
    return jax.shard_map(
        functools.partial(body, mesh.shape["exp"], mesh.shape["rep"]),
        mesh=mesh, in_specs=in_specs, out_specs=out_specs, check_vma=False,
    )
```

```python
import functools

import jax
import jax.numpy as jnp
from jax import lax
from jax.experimental import pallas as pl
from jax.experimental.pallas import tpu as pltpu
from jax.sharding import PartitionSpec as P

MESH = pl.DeviceIdType.MESH
BF = jnp.bfloat16
F32 = jnp.float32
WINDOW = 2
LAGS = (0, 1, 2, 3, 5)


def kernel(
    K, n, X, cap, S,
    tok_ref, routes_ref, combine_ref, wg_hbm, wu_hbm, wd_hbm, out_ref,
    wg, wu, wd, own, rows, ckeep, csend, crecv, xkeep, xsend, xrecv, zsend, back, picks,
    w_sem, z_s, z_r, x_s, x_r, c_s, c_r, rc_s, rc_r, rx_s, rx_r, rz_s, rz_r,
):
    T = K * n
    D = tok_ref.shape[1]
    tok_rows = tok_ref.shape[0]
    z = lax.axis_index("exp")
    r = lax.axis_index("rep")
    x, c = r // 2, r % 2

    def at_z(o):
        return {"exp": (z + o + n) % n}

    def at_x(o):
        return {"rep": ((x + o + X) % X) * 2 + c}

    sibling = {"rep": x * 2 + 1 - c}

    def remote(src, dst, send, recv, where):
        return pltpu.make_async_remote_copy(
            src_ref=src, dst_ref=dst, send_sem=send, recv_sem=recv,
            device_id=where, device_id_type=MESH,
        )

    def tile(t):
        k = t // n
        return k, jnp.where(k == K - 1, t % n + 1, t % n) % n

    def z_copy(t, i):
        return remote(own.at[t], rows.at[t, 0, 0], z_s.at[t], z_r.at[t], at_z(-i))

    def x_copy(t, o):
        return remote(rows.at[t, 0, 0], rows.at[t, o, 0], x_s.at[t, o - 1], x_r.at[t, o - 1], at_x(-o))

    def c_copy(t, o):
        return remote(rows.at[t, o, 0], rows.at[t, o, 1], c_s.at[t, o], c_r.at[t, o], sibling)

    def rc_copy(t):
        return remote(csend.at[t], crecv.at[t], rc_s.at[t], rc_r.at[t], sibling)

    def rx_copy(t, o):
        return remote(xsend.at[t, o - 1], xrecv.at[t, o - 1], rx_s.at[t, o - 1], rx_r.at[t, o - 1], at_x(o))

    def rz_copy(t, i):
        return remote(zsend.at[t], back.at[t], rz_s.at[t], rz_r.at[t], at_z(i))

    def w_copies(k):
        return [
            pltpu.make_async_copy(src.at[k], dst.at[k], w_sem.at[m, k])
            for m, (src, dst) in enumerate(((wg_hbm, wg), (wu_hbm, wu), (wd_hbm, wd)))
        ]

    barrier = pltpu.get_barrier_semaphore()
    for o in range(1, n):
        pl.semaphore_signal(barrier, inc=1, device_id=at_z(o), device_id_type=MESH)
    for o in range(1, X):
        pl.semaphore_signal(barrier, inc=1, device_id=at_x(o), device_id_type=MESH)
    pl.semaphore_signal(barrier, inc=1, device_id=sibling, device_id_type=MESH)

    for k in range(K):
        for copy in w_copies(k):
            copy.start()
    routes = jnp.transpose(jnp.concatenate([routes_ref[...]] * 4, axis=0))

    values = tok_ref[...].astype(F32)
    scale = lax.rsqrt(jnp.mean(values * values, axis=-1, keepdims=True) + 1e-05)
    normed = (values * scale).astype(BF)
    experts = n * K
    lanes = max(128, experts)
    expert_ids = lax.broadcasted_iota(jnp.int32, (tok_rows, lanes), 1)
    hot = [(routes[:, j : j + 1] == expert_ids).astype(F32) for j in range(2)]
    tri = (
        lax.broadcasted_iota(jnp.int32, (tok_rows, tok_rows), 1)
        < lax.broadcasted_iota(jnp.int32, (tok_rows, tok_rows), 0)
    ).astype(F32).astype(BF)
    before = jnp.dot(tri, (hot[0] + hot[1]).astype(BF), preferred_element_type=F32)
    slot_ids = lax.broadcasted_iota(jnp.int32, (tok_rows, T * S), 1)
    table = []
    for j in range(2):
        position = jnp.sum(before * hot[j], axis=1, keepdims=True).astype(jnp.int32)
        e = routes[:, j : j + 1]
        ze = lax.div(e, jnp.full_like(e, K))
        ke = e - ze * K
        ie = z - ze
        ie = jnp.where(ie < 0, ie + n, ie)
        ie = jnp.where(ke == K - 1, jnp.where(ie == 0, n - 1, ie - 1), ie)
        slot = (ke * n + ie) * S + position
        table.append((slot == slot_ids).astype(F32))
        picks[j] = table[j].astype(BF)
    sent = lax.dot_general(
        (table[0] + table[1]).astype(BF), normed, (((0,), (0,)), ((), ())), preferred_element_type=F32
    ).astype(BF).reshape(T, S, D)
    own[...] = sent
    own_tiles = [k * n for k in range(K - 1)] + [T - 1]
    for t in own_tiles:
        rows[t, 0, 0] = sent[t]

    def send_z(t):
        i = tile(t)[1]

        @pl.when(i > 0)
        def _():
            z_copy(t, i).start()

    pl.semaphore_wait(barrier, n + X - 1)
    for t in range(min(WINDOW, T)):
        send_z(jnp.int32(t))
    for t in own_tiles:
        for o in range(1, X):
            x_copy(t, o).start()
        c_copy(t, 0).start()

    def stage_a(t):
        i = tile(t)[1]

        @pl.when(i > 0)
        def _():
            z_copy(t, i).wait_recv()
            for o in range(1, X):
                x_copy(t, o).start()
            c_copy(t, 0).start()

        @pl.when(t + WINDOW < T)
        def _():
            send_z(t + WINDOW)

    def stage_b(t):
        for o in range(1, X):
            x_copy(t, o).wait_recv()
            c_copy(t, o).start()

    def stage_c(t):
        k = t // n

        @pl.when(t == k * n)
        def _():
            for copy in w_copies(k):
                copy.wait()

        for o in range(X):
            c_copy(t, o).wait_recv()
        a = rows[t].reshape(X * 2 * S, D)
        gate = jnp.dot(a, wg[k], preferred_element_type=F32)
        up = jnp.dot(a, wu[k], preferred_element_type=F32)
        hidden = (gate / (1.0 + jnp.exp(-gate)) * up).astype(BF)
        part = jnp.dot(hidden, wd[k], preferred_element_type=F32).reshape(X, 2, S, D)
        csend[t] = part[:, 1].astype(BF)
        rc_copy(t).start()
        ckeep[t % 4] = part[:, 0]

    def stage_d(t):
        rc_copy(t).wait_recv()
        for o in range(1, X):
            xsend[t, o - 1] = (ckeep[t % 4, o] + crecv[t, o].astype(F32)).astype(BF)
            rx_copy(t, o).start()
        xkeep[t % 4] = ckeep[t % 4, 0] + crecv[t, 0].astype(F32)

    def stage_e(t):
        i = tile(t)[1]
        total = xkeep[t % 4]
        for o in range(1, X):
            rx_copy(t, o).wait_recv()
            total = total + xrecv[t, o - 1].astype(F32)
        total = total.astype(BF)

        @pl.when(i > 0)
        def _():
            zsend[t] = total
            rz_copy(t, i).start()

        @pl.when(i == 0)
        def _():
            back[t] = total

    lag = LAGS
    stages = ((lag[0], stage_a), (lag[4], stage_e), (lag[3], stage_d), (lag[1], stage_b), (lag[2], stage_c))

    @pl.loop(0, T + max(LAGS))
    def _(tick):
        for lag, stage in stages:
            @pl.when((tick >= lag) & (tick < T + lag))
            def _(lag=lag, stage=stage):
                stage(tick - lag)

    @pl.loop(0, T)
    def _(t):
        i = tile(t)[1]

        @pl.when(i > 0)
        def _():
            rz_copy(t, i).wait_recv()

    landed = back[...].reshape(T * S, D)
    combine = jnp.transpose(jnp.concatenate([combine_ref[...]] * 4, axis=0))
    mixed = combine[:, 0:1] * jnp.dot(picks[0], landed, preferred_element_type=F32)
    mixed = mixed + combine[:, 1:2] * jnp.dot(picks[1], landed, preferred_element_type=F32)
    out_ref[...] = mixed.astype(BF)

    @pl.loop(0, T)
    def _(t):
        i = tile(t)[1]

        @pl.when(i > 0)
        def _():
            z_copy(t, i).wait_send()
            rz_copy(t, i).wait_send()

        for o in range(X):
            c_copy(t, o).wait_send()
        rc_copy(t).wait_send()
        for o in range(1, X):
            x_copy(t, o).wait_send()
            rx_copy(t, o).wait_send()


def body(n, R, tokens, routes, combine, w_gate, w_up, w_down):
    tok_rows, D = tokens.shape
    K, _, F = w_gate.shape
    X = R // 2
    cap = max(2, 3 * tok_rows // (K * n))
    S = -(-cap // 16) * 16
    T = K * n
    vmem = pl.BlockSpec(memory_space=pltpu.VMEM)
    hbm = pl.BlockSpec(memory_space=pl.ANY)
    dma = pltpu.SemaphoreType.DMA
    macs = T * X * 2 * S * D * F * 3
    return pl.pallas_call(
        functools.partial(kernel, K, n, X, cap, S),
        out_shape=jax.ShapeDtypeStruct((tok_rows, D), BF),
        in_specs=[vmem, vmem, vmem, hbm, hbm, hbm],
        out_specs=vmem,
        scratch_shapes=[
            pltpu.VMEM((K, D, F), BF),
            pltpu.VMEM((K, D, F), BF),
            pltpu.VMEM((K, F, D), BF),
            pltpu.VMEM((T, S, D), BF),
            pltpu.VMEM((T, X, 2, S, D), BF),
            pltpu.VMEM((4, X, S, D), F32),
            pltpu.VMEM((T, X, S, D), BF),
            pltpu.VMEM((T, X, S, D), BF),
            pltpu.VMEM((4, S, D), F32),
            pltpu.VMEM((T, X - 1, S, D), BF),
            pltpu.VMEM((T, X - 1, S, D), BF),
            pltpu.VMEM((T, S, D), BF),
            pltpu.VMEM((T, S, D), BF),
            pltpu.VMEM((2, tok_rows, T * S), BF),
            dma((3, K)),
            dma((T,)), dma((T,)),
            dma((T, X - 1)), dma((T, X - 1)),
            dma((T, X)), dma((T, X)),
            dma((T,)), dma((T,)),
            dma((T, X - 1)), dma((T, X - 1)),
            dma((T,)), dma((T,)),
        ],
        compiler_params=pltpu.CompilerParams(
            collective_id=0, has_side_effects=True, vmem_limit_bytes=60 * 1024 * 1024
        ),
        cost_estimate=pl.CostEstimate(flops=2 * macs, bytes_accessed=6 * K * D * F, transcendentals=T * X * 2 * S * F),
    )(tokens, routes.T, combine.T, w_gate, w_up, w_down)


def solution(mesh):
    in_specs = (
        P(("grp", "exp", "rep"), None),
        P(("grp", "exp", "rep"), None),
        P(("grp", "exp", "rep"), None),
        P("exp", None, "rep"),
        P("exp", None, "rep"),
        P("exp", "rep", None),
    )
    out_specs = P(("grp", "exp", "rep"), None)
    return jax.shard_map(
        functools.partial(body, mesh.shape["exp"], mesh.shape["rep"]),
        mesh=mesh, in_specs=in_specs, out_specs=out_specs, check_vma=False,
    )
```

```python
import functools

import jax
import jax.numpy as jnp
from jax import lax
from jax.experimental import pallas as pl
from jax.experimental.pallas import tpu as pltpu
from jax.sharding import PartitionSpec as P

MESH = pl.DeviceIdType.MESH
BF = jnp.bfloat16
F32 = jnp.float32
WINDOW = 2
LAGS = (0, 2, 3, 4, 6)


def kernel(
    K, n, X, cap, S,
    tok_ref, routes_ref, combine_ref, wg_hbm, wu_hbm, wd_hbm, out_ref,
    wg, wu, wd, own, rows, ckeep, csend, crecv, xkeep, xsend, xrecv, zsend, back, picks,
    w_sem, z_s, z_r, x_s, x_r, c_s, c_r, rc_s, rc_r, rx_s, rx_r, rz_s, rz_r,
):
    T = K * n
    D = tok_ref.shape[1]
    tok_rows = tok_ref.shape[0]
    z = lax.axis_index("exp")
    r = lax.axis_index("rep")
    x, c = r // 2, r % 2

    def at_z(o):
        return {"exp": (z + o + n) % n}

    def at_x(o):
        return {"rep": ((x + o + X) % X) * 2 + c}

    sibling = {"rep": x * 2 + 1 - c}

    def remote(src, dst, send, recv, where):
        return pltpu.make_async_remote_copy(
            src_ref=src, dst_ref=dst, send_sem=send, recv_sem=recv,
            device_id=where, device_id_type=MESH,
        )

    def tile(t):
        k = t // n
        return k, jnp.where(k == K - 1, t % n + 1, t % n) % n

    def z_copy(t, i):
        return remote(own.at[t], rows.at[t, 0, 0], z_s.at[t], z_r.at[t], at_z(-i))

    def x_copy(t, o):
        return remote(rows.at[t, 0, 0], rows.at[t, o, 0], x_s.at[t, o - 1], x_r.at[t, o - 1], at_x(-o))

    def c_copy(t, o):
        return remote(rows.at[t, o, 0], rows.at[t, o, 1], c_s.at[t, o], c_r.at[t, o], sibling)

    def rc_copy(t):
        return remote(csend.at[t], crecv.at[t], rc_s.at[t], rc_r.at[t], sibling)

    def rx_copy(t, o):
        return remote(xsend.at[t, o - 1], xrecv.at[t, o - 1], rx_s.at[t, o - 1], rx_r.at[t, o - 1], at_x(o))

    def rz_copy(t, i):
        return remote(zsend.at[t], back.at[t], rz_s.at[t], rz_r.at[t], at_z(i))

    def w_copies(k):
        return [
            pltpu.make_async_copy(src.at[k], dst.at[k], w_sem.at[m, k])
            for m, (src, dst) in enumerate(((wg_hbm, wg), (wu_hbm, wu), (wd_hbm, wd)))
        ]

    barrier = pltpu.get_barrier_semaphore()
    for o in range(1, n):
        pl.semaphore_signal(barrier, inc=1, device_id=at_z(o), device_id_type=MESH)
    for o in range(1, X):
        pl.semaphore_signal(barrier, inc=1, device_id=at_x(o), device_id_type=MESH)
    pl.semaphore_signal(barrier, inc=1, device_id=sibling, device_id_type=MESH)

    for k in range(K):
        for copy in w_copies(k):
            copy.start()
    routes = jnp.transpose(jnp.concatenate([routes_ref[...]] * 4, axis=0))

    values = tok_ref[...].astype(F32)
    scale = lax.rsqrt(jnp.mean(values * values, axis=-1, keepdims=True) + 1e-05)
    normed = (values * scale).astype(BF)
    experts = n * K
    lanes = max(128, experts)
    expert_ids = lax.broadcasted_iota(jnp.int32, (tok_rows, lanes), 1)
    hot = [(routes[:, j : j + 1] == expert_ids).astype(F32) for j in range(2)]
    tri = (
        lax.broadcasted_iota(jnp.int32, (tok_rows, tok_rows), 1)
        < lax.broadcasted_iota(jnp.int32, (tok_rows, tok_rows), 0)
    ).astype(F32).astype(BF)
    before = jnp.dot(tri, (hot[0] + hot[1]).astype(BF), preferred_element_type=F32)
    slot_ids = lax.broadcasted_iota(jnp.int32, (tok_rows, T * S), 1)
    table = []
    for j in range(2):
        position = jnp.sum(before * hot[j], axis=1, keepdims=True).astype(jnp.int32)
        e = routes[:, j : j + 1]
        ze = lax.div(e, jnp.full_like(e, K))
        ke = e - ze * K
        ie = z - ze
        ie = jnp.where(ie < 0, ie + n, ie)
        ie = jnp.where(ke == K - 1, jnp.where(ie == 0, n - 1, ie - 1), ie)
        slot = (ke * n + ie) * S + position
        table.append((slot == slot_ids).astype(F32))
        picks[j] = table[j].astype(BF)
    sent = lax.dot_general(
        (table[0] + table[1]).astype(BF), normed, (((0,), (0,)), ((), ())), preferred_element_type=F32
    ).astype(BF).reshape(T, S, D)
    own[...] = sent
    own_tiles = [k * n for k in range(K - 1)] + [T - 1]
    for t in own_tiles:
        rows[t, 0, 0] = sent[t]

    def send_z(t):
        i = tile(t)[1]

        @pl.when(i > 0)
        def _():
            z_copy(t, i).start()

    pl.semaphore_wait(barrier, n + X - 1)
    for t in range(min(WINDOW, T)):
        send_z(jnp.int32(t))
    for t in own_tiles:
        for o in range(1, X):
            x_copy(t, o).start()
        c_copy(t, 0).start()

    def stage_a(t):
        i = tile(t)[1]

        @pl.when(i > 0)
        def _():
            z_copy(t, i).wait_recv()
            for o in range(1, X):
                x_copy(t, o).start()
            c_copy(t, 0).start()

        @pl.when(t + WINDOW < T)
        def _():
            send_z(t + WINDOW)

    def stage_b(t):
        for o in range(1, X):
            x_copy(t, o).wait_recv()
            c_copy(t, o).start()

    def stage_c(t):
        k = t // n

        @pl.when(t == k * n)
        def _():
            for copy in w_copies(k):
                copy.wait()

        for o in range(X):
            c_copy(t, o).wait_recv()
        a = rows[t].reshape(X * 2 * S, D)
        gate = jnp.dot(a, wg[k], preferred_element_type=F32)
        up = jnp.dot(a, wu[k], preferred_element_type=F32)
        hidden = (gate / (1.0 + jnp.exp(-gate)) * up).astype(BF)
        part = jnp.dot(hidden, wd[k], preferred_element_type=F32).reshape(X, 2, S, D)
        csend[t] = part[:, 1].astype(BF)
        rc_copy(t).start()
        ckeep[t % 4] = part[:, 0]

    def stage_d(t):
        rc_copy(t).wait_recv()
        for o in range(1, X):
            xsend[t, o - 1] = (ckeep[t % 4, o] + crecv[t, o].astype(F32)).astype(BF)
            rx_copy(t, o).start()
        xkeep[t % 4] = ckeep[t % 4, 0] + crecv[t, 0].astype(F32)

    def stage_e(t):
        i = tile(t)[1]
        total = xkeep[t % 4]
        for o in range(1, X):
            rx_copy(t, o).wait_recv()
            total = total + xrecv[t, o - 1].astype(F32)
        total = total.astype(BF)

        @pl.when(i > 0)
        def _():
            zsend[t] = total
            rz_copy(t, i).start()

        @pl.when(i == 0)
        def _():
            back[t] = total

    stage_a(0)
    stage_b(0)
    stage_c(0)
    stage_a(1)
    stage_d(0)
    lag = LAGS
    stages = ((lag[0], 2, stage_a), (lag[4], 0, stage_e), (lag[3], 1, stage_d), (lag[1], 1, stage_b), (lag[2], 1, stage_c))

    @pl.loop(2, T + max(LAGS))
    def _(tick):
        for lag, first, stage in stages:
            @pl.when((tick >= lag + first) & (tick < T + lag))
            def _(lag=lag, stage=stage):
                stage(tick - lag)

    @pl.loop(0, T)
    def _(t):
        i = tile(t)[1]

        @pl.when(i > 0)
        def _():
            rz_copy(t, i).wait_recv()

    landed = back[...].reshape(T * S, D)
    combine = jnp.transpose(jnp.concatenate([combine_ref[...]] * 4, axis=0))
    mixed = combine[:, 0:1] * jnp.dot(picks[0], landed, preferred_element_type=F32)
    mixed = mixed + combine[:, 1:2] * jnp.dot(picks[1], landed, preferred_element_type=F32)
    out_ref[...] = mixed.astype(BF)

    @pl.loop(0, T)
    def _(t):
        i = tile(t)[1]

        @pl.when(i > 0)
        def _():
            z_copy(t, i).wait_send()
            rz_copy(t, i).wait_send()

        for o in range(X):
            c_copy(t, o).wait_send()
        rc_copy(t).wait_send()
        for o in range(1, X):
            x_copy(t, o).wait_send()
            rx_copy(t, o).wait_send()


def body(n, R, tokens, routes, combine, w_gate, w_up, w_down):
    tok_rows, D = tokens.shape
    K, _, F = w_gate.shape
    X = R // 2
    cap = max(2, 3 * tok_rows // (K * n))
    S = -(-cap // 16) * 16
    T = K * n
    vmem = pl.BlockSpec(memory_space=pltpu.VMEM)
    hbm = pl.BlockSpec(memory_space=pl.ANY)
    dma = pltpu.SemaphoreType.DMA
    macs = T * X * 2 * S * D * F * 3
    return pl.pallas_call(
        functools.partial(kernel, K, n, X, cap, S),
        out_shape=jax.ShapeDtypeStruct((tok_rows, D), BF),
        in_specs=[vmem, vmem, vmem, hbm, hbm, hbm],
        out_specs=vmem,
        scratch_shapes=[
            pltpu.VMEM((K, D, F), BF),
            pltpu.VMEM((K, D, F), BF),
            pltpu.VMEM((K, F, D), BF),
            pltpu.VMEM((T, S, D), BF),
            pltpu.VMEM((T, X, 2, S, D), BF),
            pltpu.VMEM((4, X, S, D), F32),
            pltpu.VMEM((T, X, S, D), BF),
            pltpu.VMEM((T, X, S, D), BF),
            pltpu.VMEM((4, S, D), F32),
            pltpu.VMEM((T, X - 1, S, D), BF),
            pltpu.VMEM((T, X - 1, S, D), BF),
            pltpu.VMEM((T, S, D), BF),
            pltpu.VMEM((T, S, D), BF),
            pltpu.VMEM((2, tok_rows, T * S), BF),
            dma((3, K)),
            dma((T,)), dma((T,)),
            dma((T, X - 1)), dma((T, X - 1)),
            dma((T, X)), dma((T, X)),
            dma((T,)), dma((T,)),
            dma((T, X - 1)), dma((T, X - 1)),
            dma((T,)), dma((T,)),
        ],
        compiler_params=pltpu.CompilerParams(
            collective_id=0, has_side_effects=True, vmem_limit_bytes=60 * 1024 * 1024
        ),
        cost_estimate=pl.CostEstimate(flops=2 * macs, bytes_accessed=6 * K * D * F, transcendentals=T * X * 2 * S * F),
    )(tokens, routes.T, combine.T, w_gate, w_up, w_down)


def solution(mesh):
    in_specs = (
        P(("grp", "exp", "rep"), None),
        P(("grp", "exp", "rep"), None),
        P(("grp", "exp", "rep"), None),
        P("exp", None, "rep"),
        P("exp", None, "rep"),
        P("exp", "rep", None),
    )
    out_specs = P(("grp", "exp", "rep"), None)
    return jax.shard_map(
        functools.partial(body, mesh.shape["exp"], mesh.shape["rep"]),
        mesh=mesh, in_specs=in_specs, out_specs=out_specs, check_vma=False,
    )
```

```python
import functools

import jax
import jax.numpy as jnp
from jax import lax
from jax.experimental import pallas as pl
from jax.experimental.pallas import tpu as pltpu
from jax.sharding import PartitionSpec as P

MESH = pl.DeviceIdType.MESH
BF = jnp.bfloat16
F32 = jnp.float32
WINDOW = 2
LAGS = (0, 2, 3, 4, 6)


def kernel(
    K, n, X, cap, S,
    tok_ref, routes_ref, combine_ref, wg_hbm, wu_hbm, wd_hbm, out_ref,
    wg, wu, wd, own, rows, ckeep, csend, crecv, xkeep, xsend, xrecv, zsend, back, picks,
    w_sem, z_s, z_r, x_s, x_r, c_s, c_r, rc_s, rc_r, rx_s, rx_r, rz_s, rz_r,
):
    T = K * n
    D = tok_ref.shape[1]
    tok_rows = tok_ref.shape[0]
    z = lax.axis_index("exp")
    r = lax.axis_index("rep")
    x, c = r // 2, r % 2

    def at_z(o):
        return {"exp": (z + o + n) % n}

    def at_x(o):
        return {"rep": ((x + o + X) % X) * 2 + c}

    sibling = {"rep": x * 2 + 1 - c}

    def remote(src, dst, send, recv, where):
        return pltpu.make_async_remote_copy(
            src_ref=src, dst_ref=dst, send_sem=send, recv_sem=recv,
            device_id=where, device_id_type=MESH,
        )

    def tile(t):
        k = t // n
        return k, jnp.where(k == K - 1, t % n + 1, t % n) % n

    def z_copy(t, i):
        return remote(own.at[t], rows.at[t, 0, 0], z_s.at[t], z_r.at[t], at_z(-i))

    def x_copy(t, o):
        return remote(rows.at[t, 0, 0], rows.at[t, o, 0], x_s.at[t, o - 1], x_r.at[t, o - 1], at_x(-o))

    def c_copy(t, o):
        return remote(rows.at[t, o, 0], rows.at[t, o, 1], c_s.at[t, o], c_r.at[t, o], sibling)

    def rc_copy(t):
        return remote(csend.at[t], crecv.at[t], rc_s.at[t], rc_r.at[t], sibling)

    def rx_copy(t, o):
        return remote(xsend.at[t, o - 1], xrecv.at[t, o - 1], rx_s.at[t, o - 1], rx_r.at[t, o - 1], at_x(o))

    def rz_copy(t, i):
        return remote(zsend.at[t], back.at[t], rz_s.at[t], rz_r.at[t], at_z(i))

    def w_copies(k):
        return [
            pltpu.make_async_copy(src.at[k], dst.at[k], w_sem.at[m, k])
            for m, (src, dst) in enumerate(((wg_hbm, wg), (wu_hbm, wu), (wd_hbm, wd)))
        ]

    barrier = pltpu.get_barrier_semaphore()
    for o in range(1, n):
        pl.semaphore_signal(barrier, inc=1, device_id=at_z(o), device_id_type=MESH)
    for o in range(1, X):
        pl.semaphore_signal(barrier, inc=1, device_id=at_x(o), device_id_type=MESH)
    pl.semaphore_signal(barrier, inc=1, device_id=sibling, device_id_type=MESH)

    for k in range(K):
        for copy in w_copies(k):
            copy.start()
    routes = jnp.transpose(jnp.concatenate([routes_ref[...]] * 4, axis=0))

    values = tok_ref[...].astype(F32)
    scale = lax.rsqrt(jnp.mean(values * values, axis=-1, keepdims=True) + 1e-05)
    normed = (values * scale).astype(BF)
    experts = n * K
    lanes = max(128, experts)
    expert_ids = lax.broadcasted_iota(jnp.int32, (tok_rows, lanes), 1)
    hot = [(routes[:, j : j + 1] == expert_ids).astype(F32) for j in range(2)]
    tri = (
        lax.broadcasted_iota(jnp.int32, (tok_rows, tok_rows), 1)
        < lax.broadcasted_iota(jnp.int32, (tok_rows, tok_rows), 0)
    ).astype(F32).astype(BF)
    before = jnp.dot(tri, (hot[0] + hot[1]).astype(BF), preferred_element_type=F32)
    slot_ids = lax.broadcasted_iota(jnp.int32, (tok_rows, T * S), 1)
    table = []
    for j in range(2):
        position = jnp.sum(before * hot[j], axis=1, keepdims=True).astype(jnp.int32)
        e = routes[:, j : j + 1]
        ze = lax.div(e, jnp.full_like(e, K))
        ke = e - ze * K
        ie = z - ze
        ie = jnp.where(ie < 0, ie + n, ie)
        ie = jnp.where(ke == K - 1, jnp.where(ie == 0, n - 1, ie - 1), ie)
        slot = (ke * n + ie) * S + position
        table.append((slot == slot_ids).astype(F32))
        picks[j] = table[j].astype(BF)
    sent = lax.dot_general(
        (table[0] + table[1]).astype(BF), normed, (((0,), (0,)), ((), ())), preferred_element_type=F32
    ).astype(BF).reshape(T, S, D)
    own[...] = sent
    own_tiles = [k * n for k in range(K - 1)] + [T - 1]
    for t in own_tiles:
        rows[t, 0, 0] = sent[t]

    def send_z(t):
        i = tile(t)[1]

        @pl.when(i > 0)
        def _():
            z_copy(t, i).start()

    pl.semaphore_wait(barrier, n + X - 1)
    for t in range(min(WINDOW, T)):
        send_z(jnp.int32(t))
    for t in own_tiles:
        for o in range(1, X):
            x_copy(t, o).start()
        c_copy(t, 0).start()

    def stage_a(t):
        i = tile(t)[1]

        @pl.when(i > 0)
        def _():
            z_copy(t, i).wait_recv()
            for o in range(1, X):
                x_copy(t, o).start()
            c_copy(t, 0).start()

        @pl.when(t + WINDOW < T)
        def _():
            send_z(t + WINDOW)

    def stage_b(t):
        for o in range(1, X):
            x_copy(t, o).wait_recv()
            c_copy(t, o).start()

    def stage_c(t):
        k = t // n

        @pl.when(t == k * n)
        def _():
            for copy in w_copies(k):
                copy.wait()

        for o in range(X):
            c_copy(t, o).wait_recv()
        a = rows[t].reshape(X * 2 * S, D)
        gate = jnp.dot(a, wg[k], preferred_element_type=F32)
        up = jnp.dot(a, wu[k], preferred_element_type=F32)
        hidden = (gate / (1.0 + jnp.exp(-gate)) * up).astype(BF)
        part = jnp.dot(hidden, wd[k], preferred_element_type=F32).reshape(X, 2, S, D)
        csend[t] = part[:, 1].astype(BF)
        rc_copy(t).start()
        ckeep[t % 4] = part[:, 0]

    def stage_d(t):
        rc_copy(t).wait_recv()
        for o in range(1, X):
            xsend[t, o - 1] = (ckeep[t % 4, o] + crecv[t, o].astype(F32)).astype(BF)
            rx_copy(t, o).start()
        xkeep[t % 4] = ckeep[t % 4, 0] + crecv[t, 0].astype(F32)

    def stage_e(t):
        i = tile(t)[1]
        total = xkeep[t % 4]
        for o in range(1, X):
            rx_copy(t, o).wait_recv()
            total = total + xrecv[t, o - 1].astype(F32)
        total = total.astype(BF)

        @pl.when(i > 0)
        def _():
            zsend[t] = total
            rz_copy(t, i).start()

        @pl.when(i == 0)
        def _():
            back[t] = total

    stage_a(0)
    stage_b(0)
    stage_c(0)
    stage_a(1)
    stage_d(0)
    lag = LAGS
    stages = ((lag[0], 2, stage_a), (lag[4], 0, stage_e), (lag[1], 1, stage_b), (lag[3], 1, stage_d), (lag[2], 1, stage_c))

    @pl.loop(2, T + max(LAGS))
    def _(tick):
        for lag, first, stage in stages:
            @pl.when((tick >= lag + first) & (tick < T + lag))
            def _(lag=lag, stage=stage):
                stage(tick - lag)

    @pl.loop(0, T)
    def _(t):
        i = tile(t)[1]

        @pl.when(i > 0)
        def _():
            rz_copy(t, i).wait_recv()

    landed = back[...].reshape(T * S, D)
    combine = jnp.transpose(jnp.concatenate([combine_ref[...]] * 4, axis=0))
    mixed = combine[:, 0:1] * jnp.dot(picks[0], landed, preferred_element_type=F32)
    mixed = mixed + combine[:, 1:2] * jnp.dot(picks[1], landed, preferred_element_type=F32)
    out_ref[...] = mixed.astype(BF)

    @pl.loop(0, T)
    def _(t):
        i = tile(t)[1]

        @pl.when(i > 0)
        def _():
            z_copy(t, i).wait_send()
            rz_copy(t, i).wait_send()

        for o in range(X):
            c_copy(t, o).wait_send()
        rc_copy(t).wait_send()
        for o in range(1, X):
            x_copy(t, o).wait_send()
            rx_copy(t, o).wait_send()


def body(n, R, tokens, routes, combine, w_gate, w_up, w_down):
    tok_rows, D = tokens.shape
    K, _, F = w_gate.shape
    X = R // 2
    cap = max(2, 3 * tok_rows // (K * n))
    S = -(-cap // 16) * 16
    T = K * n
    vmem = pl.BlockSpec(memory_space=pltpu.VMEM)
    hbm = pl.BlockSpec(memory_space=pl.ANY)
    dma = pltpu.SemaphoreType.DMA
    macs = T * X * 2 * S * D * F * 3
    return pl.pallas_call(
        functools.partial(kernel, K, n, X, cap, S),
        out_shape=jax.ShapeDtypeStruct((tok_rows, D), BF),
        in_specs=[vmem, vmem, vmem, hbm, hbm, hbm],
        out_specs=vmem,
        scratch_shapes=[
            pltpu.VMEM((K, D, F), BF),
            pltpu.VMEM((K, D, F), BF),
            pltpu.VMEM((K, F, D), BF),
            pltpu.VMEM((T, S, D), BF),
            pltpu.VMEM((T, X, 2, S, D), BF),
            pltpu.VMEM((4, X, S, D), F32),
            pltpu.VMEM((T, X, S, D), BF),
            pltpu.VMEM((T, X, S, D), BF),
            pltpu.VMEM((4, S, D), F32),
            pltpu.VMEM((T, X - 1, S, D), BF),
            pltpu.VMEM((T, X - 1, S, D), BF),
            pltpu.VMEM((T, S, D), BF),
            pltpu.VMEM((T, S, D), BF),
            pltpu.VMEM((2, tok_rows, T * S), BF),
            dma((3, K)),
            dma((T,)), dma((T,)),
            dma((T, X - 1)), dma((T, X - 1)),
            dma((T, X)), dma((T, X)),
            dma((T,)), dma((T,)),
            dma((T, X - 1)), dma((T, X - 1)),
            dma((T,)), dma((T,)),
        ],
        compiler_params=pltpu.CompilerParams(
            collective_id=0, has_side_effects=True, vmem_limit_bytes=60 * 1024 * 1024
        ),
        cost_estimate=pl.CostEstimate(flops=2 * macs, bytes_accessed=6 * K * D * F, transcendentals=T * X * 2 * S * F),
    )(tokens, routes.T, combine.T, w_gate, w_up, w_down)


def solution(mesh):
    in_specs = (
        P(("grp", "exp", "rep"), None),
        P(("grp", "exp", "rep"), None),
        P(("grp", "exp", "rep"), None),
        P("exp", None, "rep"),
        P("exp", None, "rep"),
        P("exp", "rep", None),
    )
    out_specs = P(("grp", "exp", "rep"), None)
    return jax.shard_map(
        functools.partial(body, mesh.shape["exp"], mesh.shape["rep"]),
        mesh=mesh, in_specs=in_specs, out_specs=out_specs, check_vma=False,
    )
```
